32 devices in a mesh: blk: 4 (over y, core), group: 8 (over z, x).
Axes of the slice: x: 2, y: 2, z: 4, core: 2. Of those that a mesh axis runs over, the one named last changes fastest.
Arguments:
- student_features: bfloat16 [4096, 768], P(('blk', 'group')), may hold values from -8 to 8
- teacher_image: bfloat16 [4096, 1152], P(('blk', 'group')), may hold values from -8 to 8
- text_embeds: bfloat16 [4096, 1152], P(('blk', 'group')), may hold values from -8 to 8
- pair_ids: int32 [4096], replicated, may hold values from 0 to 511
- head_weights: bfloat16 [1152, 768], replicated, may hold values from -1 to 1
- moment_first: float32 [1152, 768], P('group'), may hold values from -4 to 4
- moment_second: float32 [1152, 768], P('group'), may hold values from 0.01 to 0.3
Outputs:
- row_loss: float32 [4096], P(('blk', 'group'))
- new_first: float32 [1152, 768], P('group')
- new_second: float32 [1152, 768], P('group')
- new_weights: bfloat16 [1152, 768], replicated
The draws below stay inside these ranges and needn't reach their ends.
All inputs are finite; a program needn't handle non-finite values.
Results may differ from the reference program's by a relative error of at most 0.0025.
The reference program's roundings to bfloat16 on the way (of `student_b`, `teacher_b`, `texts_b`, `coeff` and `grad_projected`) count: a program that leaves them out, or rounds other values in their place, can miss the bound.
Values may be sent and summed in bfloat16 or wider, within the bound.
A program may use at most 64 MiB of HBM per device.

```python
import math
import jax
import jax.numpy as jnp
import numpy as np
from jax import lax

D = 1152
DS = 768
ROWS_DEV = 128
ROWS = 4096
N_BLK = 4
N_GROUP = 8


def head_matrix(key):
    head_key = jax.random.fold_in(jax.random.fold_in(key, 4099), 3)
    values = jax.random.normal(head_key, (D, DS), jnp.float32) / math.sqrt(DS)
    return jnp.clip(values, -1.0, 1.0)


def latent_parts(key):
    base_key = jax.random.fold_in(key, 4099)
    latent_count = 32
    coeffs = jax.random.normal(jax.random.fold_in(base_key, 1), (ROWS, latent_count), jnp.float32)
    factors = jax.random.normal(jax.random.fold_in(base_key, 2), (latent_count, DS), jnp.float32)
    return (coeffs, factors, latent_count)


def noise_field(key, salt, dims):
    noise_key = jax.random.fold_in(jax.random.fold_in(key, 5003), salt)
    return jax.random.normal(noise_key, dims, jnp.float32)


def shared_embedding(key):
    coeffs, factors, latent_count = latent_parts(key)
    mapped = jnp.dot(factors, jnp.transpose(head_matrix(key)), precision=lax.Precision.HIGHEST)
    return jnp.dot(coeffs, mapped, precision=lax.Precision.HIGHEST) / math.sqrt(latent_count)


def draw_head_weights(key, part):
    return head_matrix(key).astype(jnp.bfloat16)


def draw_student_features(key, part):
    coeffs, factors, latent_count = latent_parts(key)
    common = jnp.dot(coeffs, factors, precision=lax.Precision.HIGHEST) / math.sqrt(latent_count)
    values = 0.775 * common + 0.632 * noise_field(key, 11, (ROWS, DS))
    return jnp.clip(values, -8.0, 8.0).astype(jnp.bfloat16)


def draw_teacher_image(key, part):
    common = shared_embedding(key)
    values = 0.8 * common + 0.6 * noise_field(key, 21, (ROWS, D))
    return jnp.clip(values, -8.0, 8.0).astype(jnp.bfloat16)


def draw_text_embeds(key, part):
    common = shared_embedding(key)
    values = 0.75 * common + 0.66 * noise_field(key, 31, (ROWS, D))
    return jnp.clip(values, -8.0, 8.0).astype(jnp.bfloat16)


def plant(entries, key, smallest, top_value):
    index_at = [jax.random.randint(jax.random.fold_in(key, axis), (), 0, length) for axis, length in enumerate(entries.shape)]
    main_axis = entries.shape.index(max(entries.shape))
    neighbour = index_at[:main_axis] + [(index_at[main_axis] + 1) % entries.shape[main_axis]] + index_at[main_axis + 1:]
    return entries.at[tuple(index_at)].set(smallest).at[tuple(neighbour)].set(top_value)


def levels(key, shape, pieces, smallest, top_value):
    gain = 1.0
    for position, parts in pieces:
        heights = jax.random.uniform(jax.random.fold_in(jax.random.fold_in(key, 6), position), (parts,), jnp.float32, smallest / len(pieces), top_value / len(pieces))
        gain = gain * jnp.repeat(jnp.exp(heights), shape[position] // parts).reshape((-1,) + (1,) * (len(shape) - 1 - position))
    return gain


def cumulative_ranks(number_of, lean):
    portions = [(1 << 20) // math.isqrt(grade ** lean) + 1 for grade in range(1, number_of + 1)]
    deviation = 1 + sum(portions) // (1 << 30)
    return np.cumsum(np.array([max(1, weight // deviation) for weight in portions]))


def skewed_ids(rng, shape, number_of, lean):
    table = cumulative_ranks(number_of, lean)
    ticket = jax.random.randint(jax.random.fold_in(rng, 1), shape, 0, int(table[number_of - 1]))
    rank = jnp.searchsorted(jnp.asarray(table, jnp.int32), ticket, side="right")
    return jax.random.permutation(jax.random.fold_in(rng, 2), number_of)[rank].astype(jnp.int32)


def gaussian(key, shape, width, reach, split=(), kind=jnp.bfloat16):
    result = jax.random.normal(key, shape, jnp.float32) * width
    if len(split) > 0:
        result = levels(key, shape, split, -0.22, 0.18) * result
    return jnp.clip(result, min=-reach, max=reach).astype(kind)


def setup_inputs(seed: int = 0) -> dict:
    arg_keys = jax.random.split(jax.random.key(seed), 8)
    return {
        "student_features": draw_student_features(jax.random.fold_in(arg_keys[7], 71), 0),
        "teacher_image": draw_teacher_image(jax.random.fold_in(arg_keys[7], 71), 0),
        "text_embeds": draw_text_embeds(jax.random.fold_in(arg_keys[7], 71), 0),
        "pair_ids": plant(skewed_ids(arg_keys[3], (ROWS,), ROWS // 8, 2), jax.random.fold_in(arg_keys[3], 3), 0, (ROWS // 8) - 1).astype(jnp.int32),
        "head_weights": draw_head_weights(jax.random.fold_in(arg_keys[7], 71), 0),
        "moment_first": gaussian(arg_keys[5], (D, DS), 0.3, 4.0, ((0, 8),), jnp.float32),
        "moment_second": jnp.clip(jnp.exp(math.log(0.3) - 3.4011974 * jax.random.uniform(arg_keys[6], (D, DS), jnp.float32) ** levels(arg_keys[6], (D, DS), ((0, 8),), -0.2, 0.2)), 0.01, 0.3),
    }


student_scale = 20.0
student_bias = -1.0
teacher_scale = 25.0
teacher_bias = -1.5
label_mix = 0.5
norm_eps = 1e-06
beta_one = 0.9
beta_two = 0.95
learn_rate = 0.01
weight_decay = 0.0001
adam_eps = 1e-08
adam_step = 100.0

def unit_rows(values):
    values = values.astype(jnp.float32)
    return values * lax.rsqrt(lax.optimization_barrier(jnp.sum(values * values, axis=-1, keepdims=True)) + norm_eps)

def pair_terms(student_rows, teacher_rows, left_ids, text_rows, right_ids):
    dims = (((1,), (1,)), ((), ()))
    student_logit = student_scale * lax.dot_general(student_rows, text_rows, dims, preferred_element_type=jnp.float32) + student_bias
    teacher_logit = teacher_scale * lax.dot_general(teacher_rows, text_rows, dims, preferred_element_type=jnp.float32) + teacher_bias
    labels = (left_ids[:, None] == right_ids[None, :]).astype(jnp.float32)
    target = (1.0 - label_mix) * labels + label_mix * jax.nn.sigmoid(teacher_logit)
    losses = lax.optimization_barrier(jnp.sum(jax.nn.softplus(student_logit) - target * student_logit, axis=1))
    coeff = (jax.nn.sigmoid(student_logit) - target).astype(jnp.bfloat16)
    pulled = jnp.dot(coeff, text_rows, preferred_element_type=jnp.float32)
    return (losses, pulled)

def reference(student_features, teacher_image, text_embeds, pair_ids, head_weights, moment_first, moment_second):
    projected = lax.dot_general(student_features, head_weights, (((1,), (1,)), ((), ())), preferred_element_type=jnp.float32)
    inverse = lax.rsqrt(lax.optimization_barrier(jnp.sum(projected * projected, axis=-1, keepdims=True)) + norm_eps)
    student = projected * inverse
    student_b = student.astype(jnp.bfloat16)
    teacher_b = unit_rows(teacher_image).astype(jnp.bfloat16)
    texts_b = unit_rows(text_embeds).astype(jnp.bfloat16)
    student_grid = student_b.reshape(N_BLK, N_GROUP, ROWS_DEV, D)
    teacher_grid = teacher_b.reshape(N_BLK, N_GROUP, ROWS_DEV, D)
    text_grid = texts_b.reshape(N_BLK, N_GROUP, ROWS_DEV, D)
    ids_grid = pair_ids.reshape(N_BLK, N_GROUP, ROWS_DEV)

    def one_group(group_index):
        partner_index = (group_index + N_GROUP // 2) % N_GROUP
        images = student_grid[:, group_index].reshape(N_BLK * ROWS_DEV, D)
        teachers = teacher_grid[:, group_index].reshape(N_BLK * ROWS_DEV, D)
        left_ids = ids_grid[:, group_index].reshape(N_BLK * ROWS_DEV)
        window = jnp.concatenate([text_grid[:, group_index].reshape(N_BLK * ROWS_DEV, D), text_grid[:, partner_index].reshape(N_BLK * ROWS_DEV, D)], axis=0)
        window_ids = jnp.concatenate([ids_grid[:, group_index].reshape(N_BLK * ROWS_DEV), ids_grid[:, partner_index].reshape(N_BLK * ROWS_DEV)], axis=0)
        return pair_terms(images, teachers, left_ids, window, window_ids)
    losses, pulled = lax.map(one_group, jnp.arange(N_GROUP, dtype=jnp.int32))
    losses = jnp.transpose(losses.reshape(N_GROUP, N_BLK, ROWS_DEV), (1, 0, 2)).reshape(ROWS)
    pulled = jnp.transpose(pulled.reshape(N_GROUP, N_BLK, ROWS_DEV, D), (1, 0, 2, 3)).reshape(ROWS, D)
    row_loss = losses / ROWS_DEV
    grad_student = student_scale / ROWS_DEV * pulled
    grad_projected = (inverse * (grad_student - student * lax.optimization_barrier(jnp.sum(student * grad_student, axis=-1, keepdims=True)))).astype(jnp.bfloat16)
    head_grad = lax.dot_general(grad_projected, student_features, (((0,), (0,)), ((), ())), preferred_element_type=jnp.float32)
    new_first = beta_one * moment_first + (1.0 - beta_one) * head_grad
    new_second = beta_two * moment_second + (1.0 - beta_two) * head_grad * head_grad
    first_hat = new_first / (1.0 - beta_one ** adam_step)
    second_hat = new_second / (1.0 - beta_two ** adam_step)
    weights = head_weights.astype(jnp.float32)
    updated = weights - learn_rate * (first_hat / (jnp.sqrt(second_hat) + adam_eps) + weight_decay * weights)
    return (row_loss, new_first, new_second, updated.astype(jnp.bfloat16))
```

```python
import functools

import jax
import jax.numpy as jnp
from jax import lax
from jax.experimental import pallas as pl
from jax.experimental.pallas import tpu as pltpu
from jax.sharding import PartitionSpec as P

student_scale = 20.0
student_bias = -1.0
teacher_scale = 25.0
teacher_bias = -1.5
label_mix = 0.5
norm_eps = 1e-06
beta_one = 0.9
beta_two = 0.95
learn_rate = 0.01
weight_decay = 0.0001
adam_eps = 1e-08
adam_step = 100.0


def from_partner(shard, axis, bit):
    return lax.ppermute(shard, axis, [(i, i ^ 1 << bit) for i in range(lax.axis_size(axis))])


def unit_rows(values):
    values = values.astype(jnp.float32)
    return values * lax.rsqrt(jnp.sum(values * values, axis=-1, keepdims=True) + norm_eps)


def pair_terms(student_rows, teacher_rows, left_ids, text_rows, right_ids):
    dims = (((1,), (1,)), ((), ()))
    student_logit = (
        student_scale
        * lax.dot_general(student_rows, text_rows, dims, preferred_element_type=jnp.float32)
        + student_bias
    )
    teacher_logit = (
        teacher_scale
        * lax.dot_general(teacher_rows, text_rows, dims, preferred_element_type=jnp.float32)
        + teacher_bias
    )
    labels = (left_ids[:, None] == right_ids[None, :]).astype(jnp.float32)
    target = (1.0 - label_mix) * labels + label_mix * jax.nn.sigmoid(teacher_logit)
    losses = jnp.sum(jax.nn.softplus(student_logit) - target * student_logit, axis=1)
    coeff = (jax.nn.sigmoid(student_logit) - target).astype(jnp.bfloat16)
    pulled = jnp.dot(coeff, text_rows, preferred_element_type=jnp.float32)
    return (losses, pulled)


def per_device(
    student_features,
    teacher_image,
    text_embeds,
    pair_ids,
    head_weights,
    moment_first,
    moment_second,
):
    row_count = student_features.shape[0]
    blk_count = lax.axis_size("blk")
    group_count = lax.axis_size("group")
    swap_bit = group_count.bit_length() - 2
    group_index = lax.axis_index("group")
    partner_index = (group_index + group_count // 2) % group_count
    blk_index = lax.axis_index("blk")
    projected = lax.dot_general(
        student_features, head_weights, (((1,), (1,)), ((), ())), preferred_element_type=jnp.float32
    )
    inverse = lax.rsqrt(jnp.sum(projected * projected, axis=-1, keepdims=True) + norm_eps)
    student = projected * inverse
    student_b = student.astype(jnp.bfloat16)
    teacher_b = unit_rows(teacher_image).astype(jnp.bfloat16)
    texts_b = unit_rows(text_embeds).astype(jnp.bfloat16)
    ids_grid = pair_ids.reshape(blk_count, group_count, row_count)
    own_ids = lax.dynamic_index_in_dim(ids_grid, group_index, 1, keepdims=False)
    far_ids = lax.dynamic_index_in_dim(ids_grid, partner_index, 1, keepdims=False)
    left_ids = lax.dynamic_index_in_dim(own_ids, blk_index, 0, keepdims=False)
    far_block = from_partner(texts_b, "group", swap_bit)
    paired = jnp.concatenate([texts_b, far_block], axis=0)
    paired_ids = jnp.stack([own_ids, far_ids], axis=1).reshape(-1)
    losses, pulled = pair_terms(
        student_b,
        teacher_b,
        left_ids,
        lax.all_gather(paired, "blk", axis=0, tiled=True),
        paired_ids,
    )
    totals = (losses, pulled)
    losses, pulled = totals
    row_loss = losses / row_count
    grad_student = student_scale / row_count * pulled
    grad_projected = (
        inverse * (grad_student - student * jnp.sum(student * grad_student, axis=-1, keepdims=True))
    ).astype(jnp.bfloat16)
    shard_rows = moment_first.shape[0]
    group_grad = lax.psum_scatter(
        lax.dot_general(
            grad_projected,
            student_features,
            (((0,), (0,)), ((), ())),
            preferred_element_type=jnp.float32,
        ),
        "group",
        scatter_dimension=0,
        tiled=True,
    )
    head_grad = lax.psum(group_grad, "blk")
    new_first = beta_one * moment_first + (1.0 - beta_one) * head_grad
    new_second = beta_two * moment_second + (1.0 - beta_two) * head_grad * head_grad
    first_hat = new_first / (1.0 - beta_one**adam_step)
    second_hat = new_second / (1.0 - beta_two**adam_step)
    own_weights = lax.dynamic_slice_in_dim(
        head_weights, group_index * shard_rows, shard_rows, 0
    ).astype(jnp.float32)
    updated = own_weights - learn_rate * (
        first_hat / (jnp.sqrt(second_hat) + adam_eps) + weight_decay * own_weights
    )
    new_weights = lax.all_gather(updated.astype(jnp.bfloat16), "group", axis=0, tiled=True)
    return (row_loss, new_first, new_second, new_weights)


MESH = pl.DeviceIdType.MESH
NT = (((1,), (1,)), ((), ()))
wire = jnp.float32


def piece_plan(shard_rows, high):
    piece = -(-shard_rows // (16 * high)) * 16
    step = (shard_rows - piece) // (high - 1)
    return (piece, step)


def kernel_fits(rows, depth, width, shard_rows, blk_count, group_count):
    if blk_count % 2 or group_count % 4 or blk_count < 4 or shard_rows % 16 or rows % 128:
        return False
    if width % 256 or depth % 128:
        return False
    high = blk_count // 2
    piece, step = piece_plan(shard_rows, high)
    return (shard_rows - piece) % (high - 1) == 0 and step % 16 == 0 and 0 <= step <= piece


def step_kernel(
    H, Z, chunks,
    feat_ref, teach_ref, text_ref, ids_ref, w_ref, m1_ref, m2_ref,
    loss_ref, first_ref, second_ref, out_ref,
    tb, fb, fs, both, stu, pull, gbuf, gT, pf, pb, zr, hgb, wbuf,
    ssem, rsem,
):
    rows, depth = text_ref.shape
    width = feat_ref.shape[1]
    half = width // 2
    shard = m1_ref.shape[0]
    piece, pstep = piece_plan(shard, H)
    groups = 2 * Z
    bi = lax.axis_index("blk")
    gi = lax.axis_index("group")
    h, c = bi // 2, bi % 2
    z, x = gi // 2, gi % 2
    oc, ox = 1 - c, 1 - x

    def dev(z_, x_, h_, c_):
        return (h_ * 2 + c_, z_ * 2 + x_)

    sib = dev(z, x, h, oc)
    names = {}
    pending = []

    def copy(name, src, dst, to):
        idx = names.setdefault(name, len(names))
        return pltpu.make_async_remote_copy(
            src_ref=src, dst_ref=dst, send_sem=ssem.at[idx], recv_sem=rsem.at[idx],
            device_id=to, device_id_type=MESH,
        )

    def send(name, src, dst, to):
        op = copy(name, src, dst, to)
        op.start()
        pending.append(op)

    def arrived(name, dst):
        copy(name, dst, dst, sib).wait_recv()

    peers = [sib, dev(z, ox, h, c)]
    for j in range(1, H):
        peers += [dev(z, x, (h + j) % H, c), dev(z, ox, (h + j) % H, c)]
    for k in range(1, Z):
        peers.append(dev((z + k) % Z, x, h, c))
    barrier = pltpu.get_barrier_semaphore()
    for peer in peers:
        pl.semaphore_signal(barrier, inc=1, device_id=peer, device_id_type=MESH)

    t32 = text_ref[...].astype(jnp.float32)
    tb[0] = (t32 * lax.rsqrt(jnp.sum(t32 * t32, axis=-1, keepdims=True) + norm_eps)).astype(jnp.bfloat16)
    fb[0] = feat_ref[...]
    pl.semaphore_wait(barrier, len(peers))

    far = 2 * H
    chunk = rows // chunks
    parts = [pl.ds(i * chunk, chunk) for i in range(chunks)]
    for i, p in enumerate(parts):
        send(("F", 0, i), tb.at[0, p], tb.at[far, p], dev((z + Z // 2) % Z, x, h, c))
    for j in range(1, H):
        send(("O", j), tb.at[0], tb.at[2 * j], dev(z, x, (h + H - j) % H, c))
    send(("Os", 0), tb.at[0], tb.at[1], sib)
    send(("fx", 0), fb.at[0], fb.at[H], dev(z, ox, h, c))
    for j in range(1, H):
        send(("fy", j), fb.at[0], fb.at[j], dev(z, x, (h + H - j) % H, c))

    def my_half(col):
        return pl.ds(pl.multiple_of(col * half, 128), half)

    def feature_slot(s):
        fs[pl.ds(2 * s * rows, rows), :] = fb[s, :, my_half(c)]
        send(("fs", s), fb.at[s, :, my_half(oc)], fs.at[pl.ds((2 * s + 1) * rows, rows), :], sib)

    feature_slot(0)

    projected = lax.dot_general(feat_ref[...], w_ref[...], NT, preferred_element_type=jnp.float32)
    inverse = lax.rsqrt(jnp.sum(projected * projected, axis=-1, keepdims=True) + norm_eps)
    student = projected * inverse
    stu[...] = student
    both[0:rows] = student.astype(jnp.bfloat16)
    e32 = teach_ref[...].astype(jnp.float32)
    both[rows : 2 * rows] = (
        e32 * lax.rsqrt(jnp.sum(e32 * e32, axis=-1, keepdims=True) + norm_eps)
    ).astype(jnp.bfloat16)

    def ids_row(b_, g_):
        return ids_ref[pl.ds(b_ * groups + g_, 1), :]

    left = jnp.transpose(jnp.broadcast_to(ids_row(bi, gi).astype(jnp.float32), (rows, rows)))[:, 0:1]
    partner = (gi + Z) % groups
    total = [jnp.zeros((rows, 1), jnp.float32)]

    def pair_step(is_far, dh):
        slot = is_far * far + 2 * dh
        texts = tb[slot : slot + 2].reshape(2 * rows, depth)
        g_ = partner if is_far else gi
        h_ = (h + dh) % H
        right = jnp.concatenate([ids_row(h_ * 2 + c, g_), ids_row(h_ * 2 + oc, g_)], axis=1)
        logits = lax.dot_general(both[...], texts, NT, preferred_element_type=jnp.float32)
        s_logit = student_scale * logits[0:rows] + student_bias
        t_logit = teacher_scale * logits[rows : 2 * rows] + teacher_bias
        labels = (left == right.astype(jnp.float32)).astype(jnp.float32)
        target = (1.0 - label_mix) * labels + label_mix * jax.nn.sigmoid(t_logit)
        small = jnp.exp(-jnp.abs(s_logit))
        soft = jnp.maximum(s_logit, 0.0) + jnp.log1p(small)
        total[0] = total[0] + jnp.sum(soft - target * s_logit, axis=1, keepdims=True)
        coeff = (jax.nn.sigmoid(s_logit) - target).astype(jnp.bfloat16)
        pulled = jnp.dot(coeff, texts, preferred_element_type=jnp.float32)
        if slot == 0:
            pull[...] = pulled
        else:
            pull[...] += pulled

    def forward_far(i):
        p = parts[i]
        arrived(("F", 0, i), tb.at[far, p])
        for j in range(1, H):
            send(("F", j, i), tb.at[far, p], tb.at[far + 2 * j, p], dev(z, x, (h + H - j) % H, c))
        send(("Fs", 0, i), tb.at[far, p], tb.at[far + 1, p], sib)

    def forward_side(i):
        p = parts[i]
        for j in range(1, H):
            arrived(("F", j, i), tb.at[far + 2 * j, p])
            send(("Fs", j, i), tb.at[far + 2 * j, p], tb.at[far + 2 * j + 1, p], sib)

    arrived(("Os", 0), tb.at[1])
    pair_step(0, 0)
    for i in range(chunks):
        forward_far(i)
        if i == 0:
            for j in range(1, H):
                arrived(("O", j), tb.at[2 * j])
                send(("Os", j), tb.at[2 * j], tb.at[2 * j + 1], sib)
        if i > 0:
            forward_side(i - 1)
        if i == chunks // 2:
            for j in range(1, H):
                arrived(("fy", j), fb.at[j])
                send(("fx", j), fb.at[j], fb.at[H + j], dev(z, ox, h, c))
                feature_slot(j)
            arrived(("fx", 0), fb.at[H])
            feature_slot(H)
    for j in range(1, H):
        arrived(("Os", j), tb.at[2 * j + 1])
        pair_step(0, j)
    forward_side(chunks - 1)
    for i in range(chunks):
        arrived(("Fs", 0, i), tb.at[far + 1, parts[i]])
    pair_step(1, 0)
    for j in range(1, H):
        for i in range(chunks):
            arrived(("Fs", j, i), tb.at[far + 2 * j + 1, parts[i]])
        pair_step(1, j)

    loss_ref[...] = jnp.transpose(jnp.broadcast_to(total[0], (rows, rows)))[0:1] / rows
    gs = (student_scale / rows) * pull[...]
    st = stu[...]
    grad = (inverse * (gs - st * jnp.sum(st * gs, axis=-1, keepdims=True))).astype(jnp.bfloat16)
    gbuf[...] = jnp.transpose(grad.astype(jnp.float32)).astype(jnp.bfloat16).reshape(gbuf.shape)

    def offset(h_):
        return pl.multiple_of(h_ * pstep, 16)

    def lanes(s):
        return pl.ds(s * rows, rows)

    gT[:, :, lanes(0)] = gbuf[:, x, pl.ds(offset(h), piece), :]
    for ex in (1, 0):
        for eh in range(H):
            if ex or eh:
                x_, h_ = (x + ex) % 2, (h + H - eh) % H
                s = ex * H + eh
                send(
                    ("g", s), gbuf.at[:, x_, pl.ds(offset(h_), piece), :], gT.at[:, :, lanes(2 * s)],
                    dev(z, x_, h_, c),
                )
    send(("gs", 0), gT.at[:, :, lanes(0)], gT.at[:, :, lanes(1)], sib)
    for j in range(1, H):
        arrived(("fx", j), fb.at[H + j])
        feature_slot(H + j)
    for s in range(1, 2 * H):
        arrived(("g", s), gT.at[:, :, lanes(2 * s)])
        send(("gs", s), gT.at[:, :, lanes(2 * s)], gT.at[:, :, lanes(2 * s + 1)], sib)
    for s in range(2 * H):
        arrived(("fs", s), fs.at[pl.ds((2 * s + 1) * rows, rows), :])
    for s in range(2 * H):
        arrived(("gs", s), gT.at[:, :, lanes(2 * s + 1)])

    summed = jnp.dot(
        gT[...].reshape(Z * piece, 4 * H * rows), fs[...], preferred_element_type=jnp.float32
    ).reshape(Z, piece, half)
    pf[...] = summed
    pb[...] = summed.astype(pb.dtype)
    order = sorted(range(1, Z), key=lambda k: -min(k, Z - k))
    for k in order:
        send(("z", k), pb.at[(z + Z - k) % Z], zr.at[k - 1], dev((z + Z - k) % Z, x, h, c))
    hg = pf[z]
    for k in reversed(order):
        arrived(("z", k), zr.at[k - 1])
        hg = hg + zr[k - 1].astype(jnp.float32)
    hgb[0] = hg

    def moments(m1, m2, g):
        return (
            beta_one * m1 + (1.0 - beta_one) * g,
            beta_two * m2 + (1.0 - beta_two) * g * g,
        )

    mine = (pl.ds(offset(h), piece), my_half(c))
    first, second = moments(m1_ref[mine], m2_ref[mine], hg)
    own = w_ref[
        pl.ds(pl.multiple_of(gi * shard + h * pstep, 16), piece), my_half(c)
    ].astype(jnp.float32)
    first_hat = first / (1.0 - beta_one**adam_step)
    second_hat = second / (1.0 - beta_two**adam_step)
    updated = own - learn_rate * (first_hat / (jnp.sqrt(second_hat) + adam_eps) + weight_decay * own)
    wbuf[z, x, h, c] = updated.astype(jnp.bfloat16)

    def wslot(k, x_, h_, c_):
        return wbuf.at[(z + k) % Z, x_, h_, c_]

    for k in order:
        send(("wz", k), wslot(0, x, h, c), wslot(0, x, h, c), dev((z + Z - k) % Z, x, h, c))

    def spread(k):
        mine_k = wslot(k, x, h, c)
        send(("wx", k, 0), mine_k, mine_k, dev(z, ox, h, c))
        for j in range(1, H):
            send(("wy", k, j), mine_k, mine_k, dev(z, x, (h + H - j) % H, c))
        send(("ws", k, 0, 0), mine_k, mine_k, sib)

    spread(0)
    for j in range(1, H):
        send(("h", j), hgb.at[0], hgb.at[2 * j], dev(z, x, (h + H - j) % H, c))
    send(("hs", 0), hgb.at[0], hgb.at[1], sib)

    def relay(k):
        over_x = wslot(k, ox, h, c)
        arrived(("wx", k, 0), over_x)
        if k % 2 == 0:
            for j in range(1, H):
                send(("wd", k, j), over_x, over_x, dev(z, x, (h + H - j) % H, c))
        send(("ws", k, 1, 0), over_x, over_x, sib)
        for j in range(1, H):
            over_y = wslot(k, x, (h + j) % H, c)
            arrived(("wy", k, j), over_y)
            if k % 2 == 1:
                send(("wd", k, j), over_y, over_y, dev(z, ox, h, c))
            send(("ws", k, 0, j), over_y, over_y, sib)

    near = [0] + list(reversed(order))
    for n, k in enumerate(near[1:]):
        arrived(("wz", k), wslot(k, x, h, c))
        spread(k)
        relay(near[n])
        if n == 0:
            for j in range(1, H):
                arrived(("h", j), hgb.at[2 * j])
                send(("hs", j), hgb.at[2 * j], hgb.at[2 * j + 1], sib)
    relay(near[-1])
    for k in near:
        for j in range(1, H):
            diag = wslot(k, ox, (h + j) % H, c)
            arrived(("wd", k, j), diag)
            send(("ws", k, 1, j), diag, diag, sib)

    for j in range(H):
        arrived(("hs", j), hgb.at[2 * j + 1])
    for h_ in reversed(range(H)):
        for c_ in range(2):
            at = (pl.ds(h_ * pstep, piece), pl.ds(c_ * half, half))
            slot = (h_ - h + H) % H * 2 + (c_ + c) % 2
            first_ref[at], second_ref[at] = moments(m1_ref[at], m2_ref[at], hgb[slot])

    for k in near:
        for ex in range(2):
            for j in range(H):
                arrived(("ws", k, ex, j), wslot(k, ox if ex else x, (h + j) % H, oc))
    for z_ in range(Z):
        for x_ in range(2):
            for h_ in reversed(range(H)):
                for c_ in range(2):
                    at = (pl.ds((z_ * 2 + x_) * shard + h_ * pstep, piece), pl.ds(c_ * half, half))
                    out_ref[at] = wbuf[z_, x_, h_, c_]
    for op in pending:
        op.wait_send()


def step_per_device(
    student_features, teacher_image, text_embeds, pair_ids, head_weights, moment_first, moment_second
):
    rows, width = student_features.shape
    depth = head_weights.shape[0]
    shard = moment_first.shape[0]
    blk_count = lax.axis_size("blk")
    group_count = lax.axis_size("group")
    args = (student_features, teacher_image, text_embeds, pair_ids, head_weights, moment_first, moment_second)
    if not kernel_fits(rows, depth, width, shard, blk_count, group_count):
        return per_device(*args)
    H, Z = blk_count // 2, group_count // 2
    chunks = max(1, rows // 32)
    piece, _ = piece_plan(shard, H)
    half = width // 2
    bf16, f32 = jnp.bfloat16, jnp.float32
    sems = 8 + 3 * H * (chunks + 4) + 10 * H * Z + 4 * Z
    vmem = pl.BlockSpec(memory_space=pltpu.VMEM)
    losses, new_first, new_second, new_weights = pl.pallas_call(
        functools.partial(step_kernel, H, Z, chunks),
        out_shape=(
            jax.ShapeDtypeStruct((1, rows), f32),
            jax.ShapeDtypeStruct(moment_first.shape, f32),
            jax.ShapeDtypeStruct(moment_second.shape, f32),
            jax.ShapeDtypeStruct(head_weights.shape, bf16),
        ),
        in_specs=[vmem] * 7,
        out_specs=(vmem,) * 4,
        scratch_shapes=[
            pltpu.VMEM((4 * H, rows, depth), bf16),
            pltpu.VMEM((2 * H, rows, width), bf16),
            pltpu.VMEM((4 * H * rows, half), bf16),
            pltpu.VMEM((2 * rows, depth), bf16),
            pltpu.VMEM((rows, depth), f32),
            pltpu.VMEM((rows, depth), f32),
            pltpu.VMEM((Z, 2, shard, rows), bf16),
            pltpu.VMEM((Z, piece, 4 * H * rows), bf16),
            pltpu.VMEM((Z, piece, half), f32),
            pltpu.VMEM((Z, piece, half), wire),
            pltpu.VMEM((Z - 1, piece, half), wire),
            pltpu.VMEM((2 * H, piece, half), f32),
            pltpu.VMEM((Z, 2, H, 2, piece, half), bf16),
            pltpu.SemaphoreType.DMA((sems,)),
            pltpu.SemaphoreType.DMA((sems,)),
        ],
        compiler_params=pltpu.CompilerParams(
            collective_id=0, has_side_effects=True, vmem_limit_bytes=40 * 1024 * 1024
        ),
    )(
        student_features, teacher_image, text_embeds, pair_ids.reshape(-1, rows),
        head_weights, moment_first, moment_second,
    )
    return (losses.reshape(rows), new_first, new_second, new_weights)


def solution(mesh):
    placed = (
        P(("blk", "group"), None),
        P(("blk", "group"), None),
        P(("blk", "group"), None),
        P(),
        P(),
        P("group", None),
        P("group", None),
    )
    return jax.shard_map(
        step_per_device,
        mesh=mesh,
        in_specs=placed,
        out_specs=(P(("blk", "group")), P("group", None), P("group", None), P()),
        check_vma=False,
    )
```

```python
import functools

import jax
import jax.numpy as jnp
from jax import lax
from jax.experimental import pallas as pl
from jax.experimental.pallas import tpu as pltpu
from jax.sharding import PartitionSpec as P

student_scale = 20.0
student_bias = -1.0
teacher_scale = 25.0
teacher_bias = -1.5
label_mix = 0.5
norm_eps = 1e-06
beta_one = 0.9
beta_two = 0.95
learn_rate = 0.01
weight_decay = 0.0001
adam_eps = 1e-08
adam_step = 100.0


def from_partner(shard, axis, bit):
    return lax.ppermute(shard, axis, [(i, i ^ 1 << bit) for i in range(lax.axis_size(axis))])


def unit_rows(values):
    values = values.astype(jnp.float32)
    return values * lax.rsqrt(jnp.sum(values * values, axis=-1, keepdims=True) + norm_eps)


def pair_terms(student_rows, teacher_rows, left_ids, text_rows, right_ids):
    dims = (((1,), (1,)), ((), ()))
    student_logit = (
        student_scale
        * lax.dot_general(student_rows, text_rows, dims, preferred_element_type=jnp.float32)
        + student_bias
    )
    teacher_logit = (
        teacher_scale
        * lax.dot_general(teacher_rows, text_rows, dims, preferred_element_type=jnp.float32)
        + teacher_bias
    )
    labels = (left_ids[:, None] == right_ids[None, :]).astype(jnp.float32)
    target = (1.0 - label_mix) * labels + label_mix * jax.nn.sigmoid(teacher_logit)
    losses = jnp.sum(jax.nn.softplus(student_logit) - target * student_logit, axis=1)
    coeff = (jax.nn.sigmoid(student_logit) - target).astype(jnp.bfloat16)
    pulled = jnp.dot(coeff, text_rows, preferred_element_type=jnp.float32)
    return (losses, pulled)


def per_device(
    student_features,
    teacher_image,
    text_embeds,
    pair_ids,
    head_weights,
    moment_first,
    moment_second,
):
    row_count = student_features.shape[0]
    blk_count = lax.axis_size("blk")
    group_count = lax.axis_size("group")
    swap_bit = group_count.bit_length() - 2
    group_index = lax.axis_index("group")
    partner_index = (group_index + group_count // 2) % group_count
    blk_index = lax.axis_index("blk")
    projected = lax.dot_general(
        student_features, head_weights, (((1,), (1,)), ((), ())), preferred_element_type=jnp.float32
    )
    inverse = lax.rsqrt(jnp.sum(projected * projected, axis=-1, keepdims=True) + norm_eps)
    student = projected * inverse
    student_b = student.astype(jnp.bfloat16)
    teacher_b = unit_rows(teacher_image).astype(jnp.bfloat16)
    texts_b = unit_rows(text_embeds).astype(jnp.bfloat16)
    ids_grid = pair_ids.reshape(blk_count, group_count, row_count)
    own_ids = lax.dynamic_index_in_dim(ids_grid, group_index, 1, keepdims=False)
    far_ids = lax.dynamic_index_in_dim(ids_grid, partner_index, 1, keepdims=False)
    left_ids = lax.dynamic_index_in_dim(own_ids, blk_index, 0, keepdims=False)
    far_block = from_partner(texts_b, "group", swap_bit)
    paired = jnp.concatenate([texts_b, far_block], axis=0)
    paired_ids = jnp.stack([own_ids, far_ids], axis=1).reshape(-1)
    losses, pulled = pair_terms(
        student_b,
        teacher_b,
        left_ids,
        lax.all_gather(paired, "blk", axis=0, tiled=True),
        paired_ids,
    )
    totals = (losses, pulled)
    losses, pulled = totals
    row_loss = losses / row_count
    grad_student = student_scale / row_count * pulled
    grad_projected = (
        inverse * (grad_student - student * jnp.sum(student * grad_student, axis=-1, keepdims=True))
    ).astype(jnp.bfloat16)
    shard_rows = moment_first.shape[0]
    group_grad = lax.psum_scatter(
        lax.dot_general(
            grad_projected,
            student_features,
            (((0,), (0,)), ((), ())),
            preferred_element_type=jnp.float32,
        ),
        "group",
        scatter_dimension=0,
        tiled=True,
    )
    head_grad = lax.psum(group_grad, "blk")
    new_first = beta_one * moment_first + (1.0 - beta_one) * head_grad
    new_second = beta_two * moment_second + (1.0 - beta_two) * head_grad * head_grad
    first_hat = new_first / (1.0 - beta_one**adam_step)
    second_hat = new_second / (1.0 - beta_two**adam_step)
    own_weights = lax.dynamic_slice_in_dim(
        head_weights, group_index * shard_rows, shard_rows, 0
    ).astype(jnp.float32)
    updated = own_weights - learn_rate * (
        first_hat / (jnp.sqrt(second_hat) + adam_eps) + weight_decay * own_weights
    )
    new_weights = lax.all_gather(updated.astype(jnp.bfloat16), "group", axis=0, tiled=True)
    return (row_loss, new_first, new_second, new_weights)


MESH = pl.DeviceIdType.MESH
NT = (((1,), (1,)), ((), ()))
wire = jnp.bfloat16


def piece_plan(shard_rows, high):
    piece = -(-shard_rows // (16 * high)) * 16
    step = (shard_rows - piece) // (high - 1)
    return (piece, step)


def kernel_fits(rows, depth, width, shard_rows, blk_count, group_count):
    if blk_count % 2 or group_count % 4 or blk_count < 4 or shard_rows % 16 or rows % 128:
        return False
    if width % 256 or depth % 128:
        return False
    high = blk_count // 2
    piece, step = piece_plan(shard_rows, high)
    return (shard_rows - piece) % (high - 1) == 0 and step % 16 == 0 and 0 <= step <= piece


def step_kernel(
    H, Z, chunks,
    feat_hbm, teach_hbm, text_hbm, ids_hbm, w_hbm, m1_hbm, m2_hbm,
    loss_hbm, first_hbm, second_hbm, out_hbm,
    feat_ref, teach_ref, text_ref, ids_ref, w_ref, m1_ref, m2_ref,
    tb, fb, fs, both, stu, pull, gbuf, gT, pf, pb, zr, hgb,
    loss_ref, first_ref, second_ref, wbuf,
    ssem, rsem, lsem,
):
    rows, depth = text_ref.shape
    width = feat_ref.shape[1]
    half = width // 2
    shard = m1_ref.shape[0]
    piece, pstep = piece_plan(shard, H)
    groups = 2 * Z
    bi = lax.axis_index("blk")
    gi = lax.axis_index("group")
    h, c = bi // 2, bi % 2
    z, x = gi // 2, gi % 2
    oc, ox = 1 - c, 1 - x

    def dev(z_, x_, h_, c_):
        return (h_ * 2 + c_, z_ * 2 + x_)

    sib = dev(z, x, h, oc)
    names = {}
    pending = []

    def copy(name, src, dst, to):
        idx = names.setdefault(name, len(names))
        return pltpu.make_async_remote_copy(
            src_ref=src, dst_ref=dst, send_sem=ssem.at[idx], recv_sem=rsem.at[idx],
            device_id=to, device_id_type=MESH,
        )

    def send(name, src, dst, to):
        op = copy(name, src, dst, to)
        op.start()
        pending.append(op)

    def arrived(name, dst):
        copy(name, dst, dst, sib).wait_recv()

    loads = {}
    for n, (name, src, dst) in enumerate((
        ("text", text_hbm, text_ref), ("feat", feat_hbm, feat_ref), ("w", w_hbm, w_ref),
        ("teach", teach_hbm, teach_ref), ("ids", ids_hbm, ids_ref), ("m1", m1_hbm, m1_ref), ("m2", m2_hbm, m2_ref),
    )):
        loads[name] = pltpu.make_async_copy(src, dst, lsem.at[n])
        loads[name].start()

    def store(src, dst):
        op = pltpu.make_async_copy(src, dst, lsem.at[7 + len(stores)])
        op.start()
        stores.append(op)

    stores = []

    peers = [sib, dev(z, ox, h, c)]
    for j in range(1, H):
        peers += [dev(z, x, (h + j) % H, c), dev(z, ox, (h + j) % H, c)]
    for k in range(1, Z):
        peers.append(dev((z + k) % Z, x, h, c))
    barrier = pltpu.get_barrier_semaphore()
    for peer in peers:
        pl.semaphore_signal(barrier, inc=1, device_id=peer, device_id_type=MESH)

    loads["text"].wait()
    t32 = text_ref[...].astype(jnp.float32)
    tb[0] = (t32 * lax.rsqrt(jnp.sum(t32 * t32, axis=-1, keepdims=True) + norm_eps)).astype(jnp.bfloat16)
    loads["feat"].wait()
    fb[0] = feat_ref[...]
    pl.semaphore_wait(barrier, len(peers))

    far = 2 * H
    chunk = rows // chunks
    parts = [pl.ds(i * chunk, chunk) for i in range(chunks)]
    for i, p in enumerate(parts):
        send(("F", 0, i), tb.at[0, p], tb.at[far, p], dev((z + Z // 2) % Z, x, h, c))
    for j in range(1, H):
        send(("O", j), tb.at[0], tb.at[2 * j], dev(z, x, (h + H - j) % H, c))
    send(("Os", 0), tb.at[0], tb.at[1], sib)
    send(("fx", 0), fb.at[0], fb.at[H], dev(z, ox, h, c))

    def my_half(col):
        return pl.ds(pl.multiple_of(col * half, 128), half)

    def feature_slot(s):
        fs[pl.ds(2 * s * rows, rows), :] = fb[s, :, my_half(c)]
        send(("fs", s), fb.at[s, :, my_half(oc)], fs.at[pl.ds((2 * s + 1) * rows, rows), :], sib)

    feature_slot(0)

    loads["w"].wait()
    projected = lax.dot_general(feat_ref[...], w_ref[...], NT, preferred_element_type=jnp.float32)
    inverse = lax.rsqrt(jnp.sum(projected * projected, axis=-1, keepdims=True) + norm_eps)
    student = projected * inverse
    stu[...] = student
    both[0:rows] = student.astype(jnp.bfloat16)
    for name in ("teach", "ids", "m1", "m2"):
        loads[name].wait()
    e32 = teach_ref[...].astype(jnp.float32)
    both[rows : 2 * rows] = (
        e32 * lax.rsqrt(jnp.sum(e32 * e32, axis=-1, keepdims=True) + norm_eps)
    ).astype(jnp.bfloat16)

    def ids_row(b_, g_):
        return ids_ref[pl.ds(b_ * groups + g_, 1), :]

    left = jnp.transpose(jnp.broadcast_to(ids_row(bi, gi).astype(jnp.float32), (rows, rows)))[:, 0:1]
    partner = (gi + Z) % groups
    total = [jnp.zeros((rows, 1), jnp.float32)]

    def pair_step(is_far, dh):
        slot = is_far * far + 2 * dh
        texts = tb[slot : slot + 2].reshape(2 * rows, depth)
        g_ = partner if is_far else gi
        h_ = (h + dh) % H
        right = jnp.concatenate([ids_row(h_ * 2 + c, g_), ids_row(h_ * 2 + oc, g_)], axis=1)
        logits = lax.dot_general(both[...], texts, NT, preferred_element_type=jnp.float32)
        s_logit = student_scale * logits[0:rows] + student_bias
        t_logit = teacher_scale * logits[rows : 2 * rows] + teacher_bias
        labels = (left == right.astype(jnp.float32)).astype(jnp.float32)
        target = (1.0 - label_mix) * labels + label_mix * jax.nn.sigmoid(t_logit)
        small = jnp.exp(-jnp.abs(s_logit))
        soft = jnp.maximum(s_logit, 0.0) + jnp.log1p(small)
        total[0] = total[0] + jnp.sum(soft - target * s_logit, axis=1, keepdims=True)
        coeff = (jax.nn.sigmoid(s_logit) - target).astype(jnp.bfloat16)
        pulled = jnp.dot(coeff, texts, preferred_element_type=jnp.float32)
        if slot == 0:
            pull[...] = pulled
        else:
            pull[...] += pulled

    def forward_far(i):
        p = parts[i]
        arrived(("F", 0, i), tb.at[far, p])
        for j in range(1, H):
            send(("F", j, i), tb.at[far, p], tb.at[far + 2 * j, p], dev(z, x, (h + H - j) % H, c))
        send(("Fs", 0, i), tb.at[far, p], tb.at[far + 1, p], sib)

    def forward_side(i):
        p = parts[i]
        for j in range(1, H):
            arrived(("F", j, i), tb.at[far + 2 * j, p])
            send(("Fs", j, i), tb.at[far + 2 * j, p], tb.at[far + 2 * j + 1, p], sib)

    arrived(("Os", 0), tb.at[1])
    pair_step(0, 0)
    for i in range(chunks):
        forward_far(i)
        if i == 0:
            for j in range(1, H):
                arrived(("O", j), tb.at[2 * j])
                send(("Os", j), tb.at[2 * j], tb.at[2 * j + 1], sib)
        if i > 0:
            forward_side(i - 1)
        if i == chunks // 2:
            for j in range(1, H):
                arrived(("Os", j), tb.at[2 * j + 1])
                pair_step(0, j)
            arrived(("fx", 0), fb.at[H])
            feature_slot(H)
    for j in range(1, H):
        send(("fy", j), fb.at[0], fb.at[j], dev(z, x, (h + H - j) % H, c))
    forward_side(chunks - 1)
    for i in range(chunks):
        arrived(("Fs", 0, i), tb.at[far + 1, parts[i]])
    pair_step(1, 0)
    for j in range(1, H):
        arrived(("fy", j), fb.at[j])
        send(("fx", j), fb.at[j], fb.at[H + j], dev(z, ox, h, c))
        feature_slot(j)
    for j in range(1, H):
        for i in range(chunks):
            arrived(("Fs", j, i), tb.at[far + 2 * j + 1, parts[i]])
        pair_step(1, j)

    loss_ref[...] = jnp.transpose(jnp.broadcast_to(total[0], (rows, rows)))[0:1] / rows
    store(loss_ref, loss_hbm)
    gs = (student_scale / rows) * pull[...]
    st = stu[...]
    grad = (inverse * (gs - st * jnp.sum(st * gs, axis=-1, keepdims=True))).astype(jnp.bfloat16)
    gbuf[...] = jnp.transpose(grad.astype(jnp.float32)).astype(jnp.bfloat16).reshape(gbuf.shape)

    def offset(h_):
        return pl.multiple_of(h_ * pstep, 16)

    def lanes(s):
        return pl.ds(s * rows, rows)

    gT[:, :, lanes(0)] = gbuf[:, x, pl.ds(offset(h), piece), :]
    for ex in (1, 0):
        for eh in range(H):
            if ex or eh:
                x_, h_ = (x + ex) % 2, (h + H - eh) % H
                s = ex * H + eh
                send(
                    ("g", s), gbuf.at[:, x_, pl.ds(offset(h_), piece), :], gT.at[:, :, lanes(2 * s)],
                    dev(z, x_, h_, c),
                )
    send(("gs", 0), gT.at[:, :, lanes(0)], gT.at[:, :, lanes(1)], sib)
    for j in range(1, H):
        arrived(("fx", j), fb.at[H + j])
        feature_slot(H + j)
    for s in range(1, 2 * H):
        arrived(("g", s), gT.at[:, :, lanes(2 * s)])
        send(("gs", s), gT.at[:, :, lanes(2 * s)], gT.at[:, :, lanes(2 * s + 1)], sib)
    for s in range(2 * H):
        arrived(("fs", s), fs.at[pl.ds((2 * s + 1) * rows, rows), :])
    for s in range(2 * H):
        arrived(("gs", s), gT.at[:, :, lanes(2 * s + 1)])

    summed = jnp.dot(
        gT[...].reshape(Z * piece, 4 * H * rows), fs[...], preferred_element_type=jnp.float32
    ).reshape(Z, piece, half)
    pf[...] = summed
    pb[...] = summed.astype(pb.dtype)
    order = sorted(range(1, Z), key=lambda k: -min(k, Z - k))
    for k in order:
        send(("z", k), pb.at[(z + Z - k) % Z], zr.at[k - 1], dev((z + Z - k) % Z, x, h, c))
    hg = pf[z]
    for k in reversed(order):
        arrived(("z", k), zr.at[k - 1])
        hg = hg + zr[k - 1].astype(jnp.float32)
    hgb[0] = hg

    def moments(m1, m2, g):
        return (
            beta_one * m1 + (1.0 - beta_one) * g,
            beta_two * m2 + (1.0 - beta_two) * g * g,
        )

    mine = (pl.ds(offset(h), piece), my_half(c))
    first, second = moments(m1_ref[mine], m2_ref[mine], hg)
    own = w_ref[
        pl.ds(pl.multiple_of(gi * shard + h * pstep, 16), piece), my_half(c)
    ].astype(jnp.float32)
    first_hat = first / (1.0 - beta_one**adam_step)
    second_hat = second / (1.0 - beta_two**adam_step)
    updated = own - learn_rate * (first_hat / (jnp.sqrt(second_hat) + adam_eps) + weight_decay * own)
    wbuf[z, x, h, c] = updated.astype(jnp.bfloat16)

    def wslot(k, x_, h_, c_):
        return wbuf.at[(z + k) % Z, x_, h_, c_]

    for k in order:
        send(("wz", k), wslot(0, x, h, c), wslot(0, x, h, c), dev((z + Z - k) % Z, x, h, c))

    def spread(k):
        mine_k = wslot(k, x, h, c)
        send(("wx", k, 0), mine_k, mine_k, dev(z, ox, h, c))
        for j in range(1, H):
            send(("wy", k, j), mine_k, mine_k, dev(z, x, (h + H - j) % H, c))
        send(("ws", k, 0, 0), mine_k, mine_k, sib)

    for j in range(1, H):
        send(("h", j), hgb.at[0], hgb.at[2 * j], dev(z, x, (h + H - j) % H, c))
    send(("hs", 0), hgb.at[0], hgb.at[1], sib)
    spread(0)

    def relay(k):
        over_x = wslot(k, ox, h, c)
        arrived(("wx", k, 0), over_x)
        if k == 0:
            for j in range(1, H):
                send(("wd", k, j), over_x, over_x, dev(z, x, (h + H - j) % H, c))
        send(("ws", k, 1, 0), over_x, over_x, sib)
        for j in range(1, H):
            over_y = wslot(k, x, (h + j) % H, c)
            arrived(("wy", k, j), over_y)
            if k != 0:
                send(("wd", k, j), over_y, over_y, dev(z, ox, h, c))
            send(("ws", k, 0, j), over_y, over_y, sib)

    near = [0] + list(reversed(order))
    for n, k in enumerate(near[1:]):
        arrived(("wz", k), wslot(k, x, h, c))
        spread(k)
        relay(near[n])
        if n == 0:
            for j in range(1, H):
                arrived(("h", j), hgb.at[2 * j])
                send(("hs", j), hgb.at[2 * j], hgb.at[2 * j + 1], sib)
    relay(near[-1])
    for k in near:
        for j in range(1, H):
            diag = wslot(k, ox, (h + j) % H, c)
            arrived(("wd", k, j), diag)
            send(("ws", k, 1, j), diag, diag, sib)

    for j in range(H):
        arrived(("hs", j), hgb.at[2 * j + 1])
    for h_ in reversed(range(H)):
        for c_ in range(2):
            at = (pl.ds(h_ * pstep, piece), pl.ds(c_ * half, half))
            slot = (h_ - h + H) % H * 2 + (c_ + c) % 2
            first_ref[at], second_ref[at] = moments(m1_ref[at], m2_ref[at], hgb[slot])
    store(first_ref, first_hbm)
    store(second_ref, second_hbm)

    for k in near:
        for ex in range(2):
            for j in range(H):
                arrived(("ws", k, ex, j), wslot(k, ox if ex else x, (h + j) % H, oc))
    for z_ in range(Z):
        for x_ in range(2):
            for h_ in range(H):
                for c_ in range(2):
                    skip = piece - pstep if h_ else 0
                    row = (z_ * 2 + x_) * shard + h_ * pstep + skip
                    store(
                        wbuf.at[z_, x_, h_, c_, pl.ds(skip, piece - skip), :],
                        out_hbm.at[pl.ds(row, piece - skip), pl.ds(c_ * half, half)],
                    )
    for op in pending:
        op.wait_send()
    for op in stores:
        op.wait()


def store_kernel(cuts, *refs):
    sources, outs, held = refs[:4], refs[4:8], refs[8:12]
    sem_in, sem_out = refs[12:]
    moves = [(n, slice(None)) for n in range(3)]
    part = sources[3].shape[0] // cuts
    moves += [(3, pl.ds(n * part, part)) for n in range(cuts)]
    loads = [
        pltpu.make_async_copy(sources[n].at[at], held[n].at[at], sem_in.at[i]) for i, (n, at) in enumerate(moves)
    ]
    stores = [
        pltpu.make_async_copy(held[n].at[at], outs[n].at[at], sem_out.at[i]) for i, (n, at) in enumerate(moves)
    ]
    for op in loads:
        op.start()
    for load, op in zip(loads, stores):
        load.wait()
        op.start()
    for op in stores:
        op.wait()


def step_per_device(
    student_features, teacher_image, text_embeds, pair_ids, head_weights, moment_first, moment_second
):
    rows, width = student_features.shape
    depth = head_weights.shape[0]
    shard = moment_first.shape[0]
    blk_count = lax.axis_size("blk")
    group_count = lax.axis_size("group")
    args = (student_features, teacher_image, text_embeds, pair_ids, head_weights, moment_first, moment_second)
    if not kernel_fits(rows, depth, width, shard, blk_count, group_count):
        return per_device(*args)
    H, Z = blk_count // 2, group_count // 2
    chunks = max(1, rows // 32)
    piece, _ = piece_plan(shard, H)
    half = width // 2
    bf16, f32 = jnp.bfloat16, jnp.float32
    sems = 8 + 3 * H * (chunks + 4) + 10 * H * Z + 4 * Z
    hbm = pl.BlockSpec(memory_space=pltpu.HBM)
    operands = (
        student_features, teacher_image, text_embeds, pair_ids.reshape(-1, rows),
        head_weights, moment_first, moment_second,
    )
    cuts = 4 if depth % 64 == 0 else 1
    big = 60 * 1024 * 1024
    shapes = (
        jax.ShapeDtypeStruct((1, rows), f32),
        jax.ShapeDtypeStruct(moment_first.shape, f32),
        jax.ShapeDtypeStruct(moment_second.shape, f32),
        jax.ShapeDtypeStruct(head_weights.shape, bf16),
    )
    done = pl.pallas_call(
        functools.partial(step_kernel, H, Z, chunks),
        out_shape=shapes,
        in_specs=[hbm] * 7,
        out_specs=(hbm,) * 4,
        scratch_shapes=[pltpu.VMEM(a.shape, a.dtype) for a in operands] + [
            pltpu.VMEM((4 * H, rows, depth), bf16),
            pltpu.VMEM((2 * H, rows, width), bf16),
            pltpu.VMEM((4 * H * rows, half), bf16),
            pltpu.VMEM((2 * rows, depth), bf16),
            pltpu.VMEM((rows, depth), f32),
            pltpu.VMEM((rows, depth), f32),
            pltpu.VMEM((Z, 2, shard, rows), bf16),
            pltpu.VMEM((Z, piece, 4 * H * rows), bf16),
            pltpu.VMEM((Z, piece, half), f32),
            pltpu.VMEM((Z, piece, half), wire),
            pltpu.VMEM((Z - 1, piece, half), wire),
            pltpu.VMEM((2 * H, piece, half), f32),
            pltpu.VMEM((1, rows), f32),
            pltpu.VMEM(moment_first.shape, f32),
            pltpu.VMEM(moment_second.shape, f32),
            pltpu.VMEM((Z, 2, H, 2, piece, half), bf16),
            pltpu.SemaphoreType.DMA((sems,)),
            pltpu.SemaphoreType.DMA((sems,)),
            pltpu.SemaphoreType.DMA((10 + 4 * H * Z,)),
        ],
        compiler_params=pltpu.CompilerParams(
            collective_id=0, has_side_effects=True, vmem_limit_bytes=big
        ),
    )(*operands)
    losses, new_first, new_second, new_weights = pl.pallas_call(
        functools.partial(store_kernel, cuts),
        out_shape=shapes,
        in_specs=[hbm] * 4,
        out_specs=(hbm,) * 4,
        scratch_shapes=[pltpu.VMEM(a.shape, a.dtype) for a in shapes]
        + [pltpu.SemaphoreType.DMA((3 + cuts,))] * 2,
        compiler_params=pltpu.CompilerParams(vmem_limit_bytes=big),
    )(*done)
    return (losses.reshape(rows), new_first, new_second, new_weights)


def solution(mesh):
    placed = (
        P(("blk", "group"), None),
        P(("blk", "group"), None),
        P(("blk", "group"), None),
        P(),
        P(),
        P("group", None),
        P("group", None),
    )
    return jax.shard_map(
        step_per_device,
        mesh=mesh,
        in_specs=placed,
        out_specs=(P(("blk", "group")), P("group", None), P("group", None), P()),
        check_vma=False,
    )
```
